32 devices in a mesh: blk: 16 (over z, y, core), uly: 2 (over x).
Axes of the slice: x: 2, y: 2, z: 4, core: 2. Of those that a mesh axis runs over, the one named last changes fastest.
Arguments:
- query: bfloat16 [4096, 3072], P(('blk', 'uly')), may hold values from -40 to 40
- keys: bfloat16 [4096, 3072], P(('blk', 'uly')), may hold values from -5.2 to 5.2
- values: bfloat16 [4096, 3072], P(('blk', 'uly')), may hold values from -5 to 5
- block_mask: int32 [32, 32], P('blk'), may hold values from 0 to 1, as said below
Outputs:
- grad_query: bfloat16 [4096, 3072], P(('blk', 'uly'))
- grad_keys: bfloat16 [4096, 3072], P(('blk', 'uly'))
- grad_values: bfloat16 [4096, 3072], P(('blk', 'uly'))
The draws below stay inside these ranges and needn't reach their ends.
Inputs may be any that keep to these rules, and one draw needn't show every extreme that they name: block_mask is symmetric, its diagonal is all ones, it is zero wherever |i - j| > 2, and each row holds at most 5 ones, some rows exactly 5.
All inputs are finite; a program needn't handle non-finite values.
Results may differ from the reference program's by a relative error of at most 0.017.
Values may be sent and summed in bfloat16 or wider, within the bound.
A program may use at most 128 MiB of HBM per device.

```python
import jax
import jax.numpy as jnp
from jax import lax

HD = 128
HEADS = 24
BLK = 128
M = 5
BPD = 2
TOKENS = 4096
NB = 32


def paired_draw(key):
    first, second = jax.random.split(jax.random.fold_in(key, 4099), 2)
    shape = (TOKENS, HEADS * HD)
    query = jax.random.truncated_normal(first, -5.0, 5.0, shape, jnp.float32)
    keys = jax.random.truncated_normal(second, -5.0, 5.0, shape, jnp.float32)
    return (query, keys)


def draw_query(key, part):
    return paired_draw(key)[0].astype(jnp.bfloat16)


def draw_keys(key, part):
    return paired_draw(key)[1].astype(jnp.bfloat16)


def draw_block_mask(key, part):
    first, second = jax.random.split(jax.random.fold_in(key, 77))
    farthest = jax.random.randint(first, (), 2, BPD + 1)
    row_ids = jnp.arange(NB)[:, None]
    col_ids = jnp.arange(NB)[None, :]
    spacing = jnp.abs(col_ids - row_ids)
    lower = jnp.minimum(row_ids, col_ids)
    keep_table = jax.random.randint(second, (NB, BPD + 1), 0, 5)
    kept = keep_table[lower, jnp.minimum(spacing, BPD)] < 3
    forced = lower // (4 * BPD) % 4 == 0
    offsets = (spacing == 1) | (spacing == farthest)
    allowed = (spacing == 0) | offsets & (kept | forced)
    return allowed.astype(jnp.int32)


def levels(own_key, dims, pieces, smallest, top_value):
    gain = 1.0
    for dim, shards_of in pieces:
        steps = jax.random.uniform(jax.random.fold_in(jax.random.fold_in(own_key, 6), dim), (shards_of,), jnp.float32, smallest / len(pieces), top_value / len(pieces))
        gain = gain * jnp.repeat(jnp.exp(steps), dims[dim] // shards_of).reshape((-1,) + (1,) * (len(dims) - 1 - dim))
    return gain


def centred(stream_key, dims, spread, limit, cuts=(), kind=jnp.bfloat16):
    level = levels(stream_key, dims, cuts, -0.22, 0.18) if cuts else 1.0
    entries = jax.random.normal(stream_key, dims, jnp.float32) * spread * level
    return jnp.minimum(jnp.maximum(entries, -limit), limit).astype(kind)


def setup_inputs(seed: int = 0) -> dict:
    arg_keys = jax.random.split(jax.random.key(seed), 5)
    return {
        "query": draw_query(jax.random.fold_in(arg_keys[4], 71), 0),
        "keys": draw_keys(jax.random.fold_in(arg_keys[4], 71), 0),
        "values": centred(arg_keys[2], (TOKENS, HEADS * HD), 1.0, 5.0, ((0, 32),)),
        "block_mask": draw_block_mask(jax.random.fold_in(arg_keys[4], 71), 0),
    }


loss_scale = 64.0
masked = -1.0e30


def block_lists(rows, count):
    width = rows.shape[-1]
    running = jnp.cumsum(rows, axis=-1).astype(jnp.int32)
    ranks = jnp.arange(1, count + 1, dtype=jnp.int32)
    hits = (rows[..., None, :] == 1) & (running[..., None, :] == ranks[:, None])
    columns = jnp.arange(width, dtype=jnp.int32)
    slot_index = jnp.sum(jnp.where(hits, columns, 0), axis=-1).astype(jnp.int32)
    slot_valid = jnp.any(hits, axis=-1)
    return slot_index, slot_valid


def round_half(array):
    return lax.optimization_barrier(array.astype(jnp.bfloat16)).astype(jnp.float32)


def reference(query, keys, values, block_mask):
    scale = HD ** -0.5
    nblocks = TOKENS // BLK
    query_blocks = query.reshape(nblocks, BLK, HEADS, HD)
    key_blocks = keys.reshape(nblocks, BLK, HEADS, HD)
    value_blocks = values.reshape(nblocks, BLK, HEADS, HD)
    slot_index, slot_valid = block_lists(block_mask, M)

    def forward(block):
        chosen = slot_index[block]
        usable = slot_valid[block]
        query_one = query_blocks[block].astype(jnp.float32)
        key_tiles = key_blocks[chosen].astype(jnp.float32)
        value_tiles = value_blocks[chosen].astype(jnp.float32)
        scores = jnp.einsum('thd,muhd->htmu', query_one, key_tiles) * scale
        scores = jnp.where(usable[None, None, :, None], scores, masked)
        row_top = jnp.max(scores, axis=(2, 3))
        log_total = row_top + jnp.log(jnp.sum(jnp.exp(scores - row_top[:, :, None, None]), axis=(2, 3)))
        weights = jnp.exp(scores - log_total[:, :, None, None])
        weights_b = round_half(weights)
        attended = jnp.einsum('htmu,muhd->thd', weights_b, value_tiles)
        grad_out = (loss_scale * attended).astype(jnp.bfloat16)
        grad_float = grad_out.astype(jnp.float32)
        row_delta = jnp.transpose(jnp.sum(grad_float * attended, axis=2))
        grad_weights = jnp.einsum('thd,muhd->htmu', grad_float, value_tiles)
        grad_scores = weights * (grad_weights - row_delta[:, :, None, None])
        grad_scores_b = round_half(grad_scores)
        grad_one = (jnp.einsum('htmu,muhd->thd', grad_scores_b, key_tiles) * scale).astype(jnp.bfloat16)
        return grad_one, grad_out, log_total, row_delta

    grad_query, grad_outs, log_totals, row_deltas = lax.map(forward, jnp.arange(nblocks, dtype=jnp.int32))

    def backward(block):
        chosen = slot_index[block]
        usable = slot_valid[block]
        query_tiles = query_blocks[chosen].astype(jnp.float32)
        grad_tiles = grad_outs[chosen].astype(jnp.float32)
        total_tiles = log_totals[chosen]
        delta_tiles = row_deltas[chosen]
        key_one = key_blocks[block].astype(jnp.float32)
        value_one = value_blocks[block].astype(jnp.float32)
        scores = jnp.einsum('mthd,uhd->mhtu', query_tiles, key_one) * scale
        weights = jnp.where(usable[:, None, None, None], jnp.exp(scores - total_tiles[..., None]), 0.0)
        weights_b = round_half(weights)
        grad_value_one = jnp.einsum('mhtu,mthd->uhd', weights_b, grad_tiles).astype(jnp.bfloat16)
        grad_weights = jnp.einsum('mthd,uhd->mhtu', grad_tiles, value_one)
        grad_scores = weights * (grad_weights - delta_tiles[..., None])
        grad_scores_b = round_half(grad_scores)
        grad_key_one = (jnp.einsum('mhtu,mthd->uhd', grad_scores_b, query_tiles) * scale).astype(jnp.bfloat16)
        return grad_key_one, grad_value_one

    grad_keys, grad_values = lax.map(backward, jnp.arange(nblocks, dtype=jnp.int32))
    width = HEADS * HD
    return (grad_query.reshape(TOKENS, width), grad_keys.reshape(TOKENS, width), grad_values.reshape(TOKENS, width))
```

```python
import functools

import jax
import jax.numpy as jnp
from jax import lax
from jax.experimental import pallas as pl
from jax.experimental.pallas import tpu as pltpu
from jax.sharding import PartitionSpec as P

HD = 128
BLK = 128
CHB = 2
TEAM = 8
MESH = pl.DeviceIdType.MESH

loss_scale = 64.0
masked = -1e30
log2e = 1.4426950408889634


def dot(a, b, da, db):
    return lax.dot_general(a, b, (((da,), (db,)), ((), ())), preferred_element_type=jnp.float32)


def kernel(
    cfg,
    q_hbm, k_hbm, v_hbm, mask_ref,
    dq_hbm, dk_hbm, dv_hbm,
    qbuf, kbuf, vbuf, bbuf, bias_own, acc_k, acc_v,
    dq_st, dk_st, dv_st, gsend, grecv,
    f_send, f_recv, f_own, b_send, b_recv, m_sem,
    h_send, h_recv, r_send, r_recv, o_send, o_recv, o_own,
):
    span, ulys, teams, nh, halo, nb = cfg
    team = span * ulys
    rows = team * BLK
    hb = halo // BLK
    ch = CHB * BLK
    win = 2 * halo + ch
    wb = win // BLK
    nchunks = rows // ch
    scale = HD ** (-0.5)

    blk = lax.axis_index("blk")
    uly = lax.axis_index("uly")
    group = blk // span
    me = (blk % span) * ulys + uly
    has_lower = group > 0
    has_upper = group < teams - 1

    def device(index):
        return (group * span + index // ulys, index % ulys)

    lower = (blk - span, uly)
    upper = (blk + span, uly)

    barrier = pltpu.get_barrier_semaphore()

    def hello(d, _):
        pl.semaphore_signal(
            barrier, inc=1, device_id=device((me + d) % team), device_id_type=MESH
        )
        return 0

    lax.fori_loop(1, team, hello, 0)

    @pl.when(has_lower)
    def _():
        pl.semaphore_signal(barrier, inc=1, device_id=lower, device_id_type=MESH)

    @pl.when(has_upper)
    def _():
        pl.semaphore_signal(barrier, inc=1, device_id=upper, device_id_type=MESH)

    wpad = bias_own.shape[0]
    row_of = lax.broadcasted_iota(jnp.int32, mask_ref.shape, 0)
    own_row = jnp.sum(
        jnp.where(row_of == uly, mask_ref[...], 0).astype(jnp.float32), axis=0, keepdims=True
    )
    start = (group * team + (me // CHB) * CHB) - hb
    col = lax.broadcasted_iota(jnp.int32, (wpad, nb), 1)
    want = lax.broadcasted_iota(jnp.int32, (wpad, nb), 0) + start
    allowed = jnp.sum(
        jnp.where(col == want, jnp.broadcast_to(own_row, (wpad, nb)), 0.0), axis=1, keepdims=True
    )
    bias_own[...] = jnp.broadcast_to((1.0 - allowed) * masked, (wpad, BLK))

    beside = has_lower.astype(jnp.int32) + has_upper.astype(jnp.int32)
    pl.semaphore_wait(barrier, team - 1 + beside)

    my_rows = pl.multiple_of(me * BLK, BLK)

    def columns(owner, j):
        return pl.ds(pl.multiple_of((owner * nh + j) * HD, HD), HD)

    inputs = ((q_hbm, qbuf, 0), (k_hbm, kbuf, halo), (v_hbm, vbuf, halo))

    def push_mask(d, _):
        pltpu.make_async_remote_copy(
            src_ref=bias_own, dst_ref=bbuf.at[me], send_sem=b_send, recv_sem=b_recv,
            device_id=device((me + d) % team), device_id_type=MESH,
        ).start()
        return 0

    lax.fori_loop(1, team, push_mask, 0)

    def push_head(j, _):
        for a, (src, dst, offset) in enumerate(inputs):
            pltpu.make_async_copy(
                src.at[:, columns(me, j)],
                dst.at[j, pl.ds(my_rows + offset, BLK), :],
                f_own.at[a, j],
            ).start()

        def push_peer(d, _):
            peer = (me + d) % team
            for a, (src, dst, offset) in enumerate(inputs):
                pltpu.make_async_remote_copy(
                    src_ref=src.at[:, columns(peer, j)],
                    dst_ref=dst.at[j, pl.ds(my_rows + offset, BLK), :],
                    send_sem=f_send.at[a, j], recv_sem=f_recv.at[a, j],
                    device_id=device(peer), device_id_type=MESH,
                ).start()
            return 0

        lax.fori_loop(1, team, push_peer, 0)
        return 0

    lax.fori_loop(0, nh, push_head, 0)

    own_bias = pltpu.make_async_copy(bias_own, bbuf.at[me], m_sem)
    own_bias.start()
    own_bias.wait()

    acc_k[...] = jnp.zeros_like(acc_k)
    acc_v[...] = jnp.zeros_like(acc_v)
    edge = jnp.zeros((nh, halo, HD), jnp.bfloat16)

    @pl.when(jnp.logical_not(has_lower))
    def _():
        kbuf[:, 0:halo, :] = edge
        vbuf[:, 0:halo, :] = edge

    @pl.when(jnp.logical_not(has_upper))
    def _():
        kbuf[:, halo + rows :, :] = edge
        vbuf[:, halo + rows :, :] = edge

    def drain(ref, sem):
        pltpu.make_async_copy(ref, ref, sem).wait()

    peers_rows = (team - 1) * BLK
    drain(bbuf.at[pl.ds(0, team - 1)], b_recv)

    def halo_copies(j, side):
        place = halo if side == 0 else rows
        land = halo + rows if side == 0 else 0
        return [
            pltpu.make_async_remote_copy(
                src_ref=buf.at[j, pl.ds(place, halo), :],
                dst_ref=buf.at[j, pl.ds(land, halo), :],
                send_sem=h_send.at[a, j, side], recv_sem=h_recv.at[a, j, side],
                device_id=lower if side == 0 else upper, device_id_type=MESH,
            )
            for a, buf in enumerate((kbuf, vbuf))
        ]

    def grad_copies(j, side):
        return [
            pltpu.make_async_remote_copy(
                src_ref=gsend.at[a, j, side], dst_ref=grecv.at[a, j, side],
                send_sem=r_send.at[a, j, side], recv_sem=r_recv.at[a, j, side],
                device_id=lower if side == 0 else upper, device_id_type=MESH,
            )
            for a in range(2)
        ]

    there = (has_lower, has_upper)

    def send_block(a, j, block):
        st, out = ((dq_st, dq_hbm), (dk_st, dk_hbm), (dv_st, dv_hbm))[a]
        src = st.at[j, pl.ds(block * BLK, BLK), :]
        dst = out.at[:, columns(me, j)]

        @pl.when(me == block)
        def _():
            pltpu.make_async_copy(src, dst, o_own.at[a, j]).start()

        @pl.when(me != block)
        def _():
            pltpu.make_async_remote_copy(
                src_ref=src, dst_ref=dst, send_sem=o_send.at[a, j], recv_sem=o_recv.at[a, j],
                device_id=device(block), device_id_type=MESH,
            ).start()

    def chunk(j, c):
        base = c * ch
        k = kbuf[j, base : base + win, :]
        v = vbuf[j, base : base + win, :]
        q = qbuf[j, base : base + ch, :]
        bias = jnp.concatenate([bbuf[c * CHB + i] for i in range(CHB)], axis=1)[:wb]
        s = dot(k, q, 1, 1).reshape(wb, BLK, ch) * (scale * log2e) + bias[:, None, :]
        top = jnp.max(jnp.max(s, axis=0), axis=0, keepdims=True)
        p = jnp.exp2(s - top[None])
        total = jnp.sum(jnp.sum(p, axis=0), axis=0, keepdims=True)
        p = p.reshape(win, ch)
        pb = p.astype(jnp.bfloat16)
        inv = 1.0 / total
        o = dot(v, pb, 0, 0) * inv
        g = (loss_scale * o * inv).astype(jnp.bfloat16)
        delta = jnp.sum(g.astype(jnp.float32) * o, axis=0, keepdims=True)
        acc_v[j, base : base + win, :] += dot(pb, g, 1, 1)
        ds = (p * (dot(v, g, 1, 0) - delta)).astype(jnp.bfloat16)
        acc_k[j, base : base + win, :] += dot(ds, q, 1, 0)
        dq = dot(k, ds, 0, 0) * scale
        dq_st[j, base : base + ch, :] = dq.T.astype(jnp.bfloat16)
        for i in range(CHB):
            send_block(0, j, c * CHB + i)

    def finish_block(j, block):
        at = halo + block * BLK
        here = slice(block * BLK, (block + 1) * BLK)
        dk_st[j, here, :] = (acc_k[j, at : at + BLK, :] * scale).astype(jnp.bfloat16)
        dv_st[j, here, :] = acc_v[j, at : at + BLK, :].astype(jnp.bfloat16)
        send_block(1, j, block)
        send_block(2, j, block)

    inner_blocks = [b for b in range(team) if hb <= b < team - hb]
    outer_blocks = [b for b in range(team) if b not in inner_blocks]
    inner_chunks = [c for c in range(nchunks) if c * ch >= halo and c * ch + ch + halo <= rows]
    outer_chunks = [c for c in range(nchunks) if c not in inner_chunks]

    def finish_outer(j):
        for side in range(2):
            @pl.when(there[1 - side])
            def _():
                for copy in grad_copies(j, side):
                    copy.wait_recv()
                at = halo if side == 1 else rows
                acc_k[j, at : at + halo, :] += grecv[0, j, side].astype(jnp.float32)
                acc_v[j, at : at + halo, :] += grecv[1, j, side].astype(jnp.float32)

        for block in outer_blocks:
            finish_block(j, block)

    def head(j, _):
        for a, (src, dst, offset) in enumerate(inputs):
            drain(dst.at[j, pl.ds(offset, peers_rows), :], f_recv.at[a, j])
            drain(dst.at[j, pl.ds(offset, BLK), :], f_own.at[a, j])
        for side in range(2):
            @pl.when(there[side])
            def _():
                for copy in halo_copies(j, side):
                    copy.start()

        for c in inner_chunks:
            chunk(j, c)

        @pl.when(j > 0)
        def _():
            finish_outer(j - 1)

        for side in range(2):
            @pl.when(there[1 - side])
            def _():
                for copy in halo_copies(j, side):
                    copy.wait_recv()

        for c in outer_chunks:
            chunk(j, c)

        for side in range(2):
            @pl.when(there[side])
            def _():
                at = 0 if side == 0 else halo + rows
                gsend[0, j, side] = acc_k[j, at : at + halo, :].astype(jnp.bfloat16)
                gsend[1, j, side] = acc_v[j, at : at + halo, :].astype(jnp.bfloat16)
                for copy in grad_copies(j, side):
                    copy.start()

        for block in inner_blocks:
            finish_block(j, block)
        return 0

    lax.fori_loop(0, nh, head, 0)
    finish_outer(nh - 1)

    drain(bbuf.at[pl.ds(0, team - 1)], b_send)

    def settle(j, _):
        for a, (src, dst, offset) in enumerate(inputs):
            drain(dst.at[j, pl.ds(offset, peers_rows), :], f_send.at[a, j])
        for side in range(2):
            @pl.when(there[side])
            def _():
                for copy in halo_copies(j, side) + grad_copies(j, side):
                    copy.wait_send()

        for a, st in enumerate((dq_st, dk_st, dv_st)):
            drain(st.at[j, pl.ds(0, peers_rows), :], o_send.at[a, j])
            drain(st.at[j, pl.ds(0, BLK), :], o_own.at[a, j])
            drain(st.at[j, pl.ds(0, peers_rows), :], o_recv.at[a, j])
        return 0

    lax.fori_loop(0, nh, settle, 0)


def body(query, keys, values, block_mask):
    blks = lax.axis_size("blk")
    ulys = lax.axis_size("uly")
    heads_all = query.shape[1] // HD
    span = max(1, TEAM // ulys)
    team = span * ulys
    nh = heads_all // team
    halo = query.shape[0] * ulys
    rows = team * BLK
    nb = block_mask.shape[1]
    cfg = (span, ulys, blks // span, nh, halo, nb)
    wpad = -(-(2 * halo // BLK + CHB) // 8) * 8
    bf, f32 = jnp.bfloat16, jnp.float32
    dma = pltpu.SemaphoreType.DMA
    anywhere = pl.BlockSpec(memory_space=pl.ANY)
    return pl.pallas_call(
        functools.partial(kernel, cfg),
        out_shape=[jax.ShapeDtypeStruct(query.shape, bf)] * 3,
        in_specs=[anywhere] * 3 + [pl.BlockSpec(memory_space=pltpu.VMEM)],
        out_specs=[anywhere] * 3,
        scratch_shapes=[
            pltpu.VMEM((nh, rows, HD), bf),
            pltpu.VMEM((nh, rows + 2 * halo, HD), bf),
            pltpu.VMEM((nh, rows + 2 * halo, HD), bf),
            pltpu.VMEM((team, wpad, BLK), f32),
            pltpu.VMEM((wpad, BLK), f32),
            pltpu.VMEM((nh, rows + 2 * halo, HD), f32),
            pltpu.VMEM((nh, rows + 2 * halo, HD), f32),
            pltpu.VMEM((nh, rows, HD), bf),
            pltpu.VMEM((nh, rows, HD), bf),
            pltpu.VMEM((nh, rows, HD), bf),
            pltpu.VMEM((2, nh, 2, halo, HD), bf),
            pltpu.VMEM((2, nh, 2, halo, HD), bf),
            dma((3, nh)), dma((3, nh)), dma((3, nh)),
            dma, dma, dma,
            dma((2, nh, 2)), dma((2, nh, 2)), dma((2, nh, 2)), dma((2, nh, 2)),
            dma((3, nh)), dma((3, nh)), dma((3, nh)),
        ],
        compiler_params=pltpu.CompilerParams(
            collective_id=0, has_side_effects=True, vmem_limit_bytes=56 * 1024 * 1024
        ),
    )(query, keys, values, block_mask)


def solution(mesh):
    in_specs = (
        P(("blk", "uly"), None),
        P(("blk", "uly"), None),
        P(("blk", "uly"), None),
        P("blk", None),
    )
    out_specs = (P(("blk", "uly"), None), P(("blk", "uly"), None), P(("blk", "uly"), None))
    return jax.shard_map(body, mesh=mesh, in_specs=in_specs, out_specs=out_specs, check_vma=False)
```

```python
import functools

import jax
import jax.numpy as jnp
from jax import lax
from jax.experimental import pallas as pl
from jax.experimental.pallas import tpu as pltpu
from jax.sharding import PartitionSpec as P

HD = 128
BLK = 128
CHB = 2
PIECES = 4
TEAM = 8
MESH = pl.DeviceIdType.MESH

loss_scale = 64.0
masked = -1e30
log2e = 1.4426950408889634


def dot(a, b, da, db):
    return lax.dot_general(a, b, (((da,), (db,)), ((), ())), preferred_element_type=jnp.float32)


def kernel(
    cfg,
    q_hbm, k_hbm, v_hbm, mask_ref,
    dq_hbm, dk_hbm, dv_hbm,
    qbuf, kbuf, vbuf, bbuf, bias_own, acc_k, acc_v,
    dq_st, dk_st, dv_st, gsend, grecv,
    f_send, f_recv, f_own, b_send, b_recv, m_sem,
    h_send, h_recv, r_send, r_recv, o_send, o_recv, o_own,
):
    span, ulys, teams, nh, halo, nb = cfg
    team = span * ulys
    rows = team * BLK
    hb = halo // BLK
    ch = CHB * BLK
    win = 2 * halo + ch
    wb = win // BLK
    nchunks = rows // ch
    scale = HD ** (-0.5)

    blk = lax.axis_index("blk")
    uly = lax.axis_index("uly")
    group = blk // span
    me = (blk % span) * ulys + uly
    has_lower = group > 0
    has_upper = group < teams - 1

    def device(index):
        return (group * span + index // ulys, index % ulys)

    lower = (blk - span, uly)
    upper = (blk + span, uly)

    barrier = pltpu.get_barrier_semaphore()

    def hello(d, _):
        pl.semaphore_signal(
            barrier, inc=1, device_id=device((me + d) % team), device_id_type=MESH
        )
        return 0

    lax.fori_loop(1, team, hello, 0)

    @pl.when(has_lower)
    def _():
        pl.semaphore_signal(barrier, inc=1, device_id=lower, device_id_type=MESH)

    @pl.when(has_upper)
    def _():
        pl.semaphore_signal(barrier, inc=1, device_id=upper, device_id_type=MESH)

    wpad = bias_own.shape[0]
    row_of = lax.broadcasted_iota(jnp.int32, mask_ref.shape, 0)
    own_row = jnp.sum(
        jnp.where(row_of == uly, mask_ref[...], 0).astype(jnp.float32), axis=0, keepdims=True
    )
    start = (group * team + (me // CHB) * CHB) - hb
    col = lax.broadcasted_iota(jnp.int32, (wpad, nb), 1)
    want = lax.broadcasted_iota(jnp.int32, (wpad, nb), 0) + start
    allowed = jnp.sum(
        jnp.where(col == want, jnp.broadcast_to(own_row, (wpad, nb)), 0.0), axis=1, keepdims=True
    )
    bias_own[...] = jnp.broadcast_to((1.0 - allowed) * masked, (wpad, BLK))

    beside = has_lower.astype(jnp.int32) + has_upper.astype(jnp.int32)
    pl.semaphore_wait(barrier, team - 1 + beside)

    my_rows = pl.multiple_of(me * BLK, BLK)

    def columns(owner, j):
        return pl.ds(pl.multiple_of((owner * nh + j) * HD, HD), HD)

    inputs = ((q_hbm, qbuf, 0), (k_hbm, kbuf, halo), (v_hbm, vbuf, halo))

    def push_mask(d, _):
        pltpu.make_async_remote_copy(
            src_ref=bias_own, dst_ref=bbuf.at[me], send_sem=b_send, recv_sem=b_recv,
            device_id=device((me + d) % team), device_id_type=MESH,
        ).start()
        return 0

    lax.fori_loop(1, team, push_mask, 0)

    def push_head(j, _):
        for a, (src, dst, offset) in enumerate(inputs):
            pltpu.make_async_copy(
                src.at[:, columns(me, j)],
                dst.at[j, pl.ds(my_rows + offset, BLK), :],
                f_own.at[a, j],
            ).start()

        def push_peer(d, _):
            peer = (me + d) % team
            for a, (src, dst, offset) in enumerate(inputs):
                pltpu.make_async_remote_copy(
                    src_ref=src.at[:, columns(peer, j)],
                    dst_ref=dst.at[j, pl.ds(my_rows + offset, BLK), :],
                    send_sem=f_send.at[a, j], recv_sem=f_recv.at[a, j],
                    device_id=device(peer), device_id_type=MESH,
                ).start()
            return 0

        lax.fori_loop(1, team, push_peer, 0)
        return 0

    lax.fori_loop(0, nh, push_head, 0)

    own_bias = pltpu.make_async_copy(bias_own, bbuf.at[me], m_sem)
    own_bias.start()
    own_bias.wait()

    acc_k[...] = jnp.zeros_like(acc_k)
    acc_v[...] = jnp.zeros_like(acc_v)
    edge = jnp.zeros((nh, halo, HD), jnp.bfloat16)

    @pl.when(jnp.logical_not(has_lower))
    def _():
        kbuf[:, 0:halo, :] = edge
        vbuf[:, 0:halo, :] = edge

    @pl.when(jnp.logical_not(has_upper))
    def _():
        kbuf[:, halo + rows :, :] = edge
        vbuf[:, halo + rows :, :] = edge

    def drain(ref, sem):
        pltpu.make_async_copy(ref, ref, sem).wait()

    peers_rows = (team - 1) * BLK
    drain(bbuf.at[pl.ds(0, team - 1)], b_recv)

    def halo_copies(j, side):
        place = halo if side == 0 else rows
        land = halo + rows if side == 0 else 0
        return [
            pltpu.make_async_remote_copy(
                src_ref=buf.at[j, pl.ds(place, halo), :],
                dst_ref=buf.at[j, pl.ds(land, halo), :],
                send_sem=h_send.at[a, j, side], recv_sem=h_recv.at[a, j, side],
                device_id=lower if side == 0 else upper, device_id_type=MESH,
            )
            for a, buf in enumerate((kbuf, vbuf))
        ]

    def grad_copies(j, side):
        return [
            pltpu.make_async_remote_copy(
                src_ref=gsend.at[a, j, side], dst_ref=grecv.at[a, j, side],
                send_sem=r_send.at[a, j, side], recv_sem=r_recv.at[a, j, side],
                device_id=lower if side == 0 else upper, device_id_type=MESH,
            )
            for a in range(2)
        ]

    there = (has_lower, has_upper)

    def send_block(a, j, block):
        st, out = ((dq_st, dq_hbm), (dk_st, dk_hbm), (dv_st, dv_hbm))[a]
        src = st.at[j, pl.ds(block * BLK, BLK), :]
        dst = out.at[:, columns(me, j)]

        @pl.when(me == block)
        def _():
            pltpu.make_async_copy(src, dst, o_own.at[a, j]).start()

        @pl.when(me != block)
        def _():
            pltpu.make_async_remote_copy(
                src_ref=src, dst_ref=dst, send_sem=o_send.at[a, j], recv_sem=o_recv.at[a, j],
                device_id=device(block), device_id_type=MESH,
            ).start()

    def chunk(j, c):
        base = c * ch
        k = kbuf[j, base : base + win, :]
        v = vbuf[j, base : base + win, :]
        q = qbuf[j, base : base + ch, :]
        bias = jnp.concatenate([bbuf[c * CHB + i] for i in range(CHB)], axis=1)[:wb]
        s = dot(k, q, 1, 1).reshape(wb, BLK, ch) * (scale * log2e) + bias[:, None, :]
        top = jnp.max(jnp.max(s, axis=0), axis=0, keepdims=True)
        p = jnp.exp2(s - top[None])
        total = jnp.sum(jnp.sum(p, axis=0), axis=0, keepdims=True)
        p = p.reshape(win, ch)
        pb = p.astype(jnp.bfloat16)
        inv = 1.0 / total
        o = dot(v, pb, 0, 0) * inv
        g = (loss_scale * o * inv).astype(jnp.bfloat16)
        delta = jnp.sum(g.astype(jnp.float32) * o, axis=0, keepdims=True)
        acc_v[j, base : base + win, :] += dot(pb, g, 1, 1)
        ds = (p * (dot(v, g, 1, 0) - delta)).astype(jnp.bfloat16)
        acc_k[j, base : base + win, :] += dot(ds, q, 1, 0)
        dq = dot(k, ds, 0, 0) * scale
        dq_st[j, base : base + ch, :] = dq.T.astype(jnp.bfloat16)
        for i in range(CHB):
            send_block(0, j, c * CHB + i)

    def finish_block(j, block):
        at = halo + block * BLK
        here = slice(block * BLK, (block + 1) * BLK)
        dk_st[j, here, :] = (acc_k[j, at : at + BLK, :] * scale).astype(jnp.bfloat16)
        dv_st[j, here, :] = acc_v[j, at : at + BLK, :].astype(jnp.bfloat16)
        send_block(1, j, block)
        send_block(2, j, block)

    inner_blocks = [b for b in range(team) if hb <= b < team - hb]
    outer_blocks = [b for b in range(team) if b not in inner_blocks]
    inner_chunks = [c for c in range(nchunks) if c * ch >= halo and c * ch + ch + halo <= rows]
    outer_chunks = [c for c in range(nchunks) if c not in inner_chunks]

    def finish_outer(j):
        for side in range(2):
            @pl.when(there[1 - side])
            def _():
                for copy in grad_copies(j, side):
                    copy.wait_recv()
                at = halo if side == 1 else rows
                acc_k[j, at : at + halo, :] += grecv[0, j, side].astype(jnp.float32)
                acc_v[j, at : at + halo, :] += grecv[1, j, side].astype(jnp.float32)

        for block in outer_blocks:
            finish_block(j, block)

    def head(j, _):
        for a, (src, dst, offset) in enumerate(inputs):
            drain(dst.at[j, pl.ds(offset, peers_rows), :], f_recv.at[a, j])
            drain(dst.at[j, pl.ds(offset, BLK), :], f_own.at[a, j])
        for side in range(2):
            @pl.when(there[side])
            def _():
                for copy in halo_copies(j, side):
                    copy.start()

        for c in inner_chunks:
            chunk(j, c)

        @pl.when(j > 0)
        def _():
            finish_outer(j - 1)

        for side in range(2):
            @pl.when(there[1 - side])
            def _():
                for copy in halo_copies(j, side):
                    copy.wait_recv()

        for c in outer_chunks:
            chunk(j, c)

        for side in range(2):
            @pl.when(there[side])
            def _():
                at = 0 if side == 0 else halo + rows
                gsend[0, j, side] = acc_k[j, at : at + halo, :].astype(jnp.bfloat16)
                gsend[1, j, side] = acc_v[j, at : at + halo, :].astype(jnp.bfloat16)
                for copy in grad_copies(j, side):
                    copy.start()

        for block in inner_blocks:
            finish_block(j, block)
        return 0

    lax.fori_loop(0, nh, head, 0)
    finish_outer(nh - 1)

    drain(bbuf.at[pl.ds(0, team - 1)], b_send)

    def settle(j, _):
        for a, (src, dst, offset) in enumerate(inputs):
            drain(dst.at[j, pl.ds(offset, peers_rows), :], f_send.at[a, j])
        for side in range(2):
            @pl.when(there[side])
            def _():
                for copy in halo_copies(j, side) + grad_copies(j, side):
                    copy.wait_send()

        for a, st in enumerate((dq_st, dk_st, dv_st)):
            drain(st.at[j, pl.ds(0, peers_rows), :], o_send.at[a, j])
            drain(st.at[j, pl.ds(0, BLK), :], o_own.at[a, j])
            drain(st.at[j, pl.ds(0, peers_rows), :], o_recv.at[a, j])
        return 0

    lax.fori_loop(0, nh, settle, 0)


def write_out(*refs):
    n = (len(refs) - 2) // 2
    srcs, dsts, held, sem = refs[:n], refs[n : 2 * n], refs[2 * n], refs[2 * n + 1]
    loads, stores = [], []
    for a, (src, dst) in enumerate(zip(srcs, dsts)):
        step = src.shape[0] // PIECES
        for i in range(PIECES):
            here = pl.ds(i * step, step)
            loads.append(pltpu.make_async_copy(src.at[here], held.at[a, here], sem.at[0, a, i]))
            stores.append(pltpu.make_async_copy(held.at[a, here], dst.at[here], sem.at[1, a, i]))
    for load in loads:
        load.start()
    for load, store in zip(loads, stores):
        load.wait()
        store.start()
    for store in stores:
        store.wait()


def written(*arrays):
    anywhere = pl.BlockSpec(memory_space=pl.ANY)
    return pl.pallas_call(
        write_out,
        out_shape=[jax.ShapeDtypeStruct(a.shape, a.dtype) for a in arrays],
        in_specs=[anywhere] * len(arrays),
        out_specs=[anywhere] * len(arrays),
        scratch_shapes=[
            pltpu.VMEM((len(arrays),) + arrays[0].shape, arrays[0].dtype),
            pltpu.SemaphoreType.DMA((2, len(arrays), PIECES)),
        ],
    )(*arrays)


def body(query, keys, values, block_mask):
    blks = lax.axis_size("blk")
    ulys = lax.axis_size("uly")
    heads_all = query.shape[1] // HD
    span = max(1, TEAM // ulys)
    team = span * ulys
    nh = heads_all // team
    halo = query.shape[0] * ulys
    rows = team * BLK
    nb = block_mask.shape[1]
    cfg = (span, ulys, blks // span, nh, halo, nb)
    wpad = -(-(2 * halo // BLK + CHB) // 8) * 8
    bf, f32 = jnp.bfloat16, jnp.float32
    dma = pltpu.SemaphoreType.DMA
    anywhere = pl.BlockSpec(memory_space=pl.ANY)
    grads = pl.pallas_call(
        functools.partial(kernel, cfg),
        out_shape=[jax.ShapeDtypeStruct(query.shape, bf)] * 3,
        in_specs=[anywhere] * 3 + [pl.BlockSpec(memory_space=pltpu.VMEM)],
        out_specs=[anywhere] * 3,
        scratch_shapes=[
            pltpu.VMEM((nh, rows, HD), bf),
            pltpu.VMEM((nh, rows + 2 * halo, HD), bf),
            pltpu.VMEM((nh, rows + 2 * halo, HD), bf),
            pltpu.VMEM((team, wpad, BLK), f32),
            pltpu.VMEM((wpad, BLK), f32),
            pltpu.VMEM((nh, rows + 2 * halo, HD), f32),
            pltpu.VMEM((nh, rows + 2 * halo, HD), f32),
            pltpu.VMEM((nh, rows, HD), bf),
            pltpu.VMEM((nh, rows, HD), bf),
            pltpu.VMEM((nh, rows, HD), bf),
            pltpu.VMEM((2, nh, 2, halo, HD), bf),
            pltpu.VMEM((2, nh, 2, halo, HD), bf),
            dma((3, nh)), dma((3, nh)), dma((3, nh)),
            dma, dma, dma,
            dma((2, nh, 2)), dma((2, nh, 2)), dma((2, nh, 2)), dma((2, nh, 2)),
            dma((3, nh)), dma((3, nh)), dma((3, nh)),
        ],
        compiler_params=pltpu.CompilerParams(
            collective_id=0, has_side_effects=True, vmem_limit_bytes=56 * 1024 * 1024
        ),
    )(query, keys, values, block_mask)
    return written(*grads)


def solution(mesh):
    in_specs = (
        P(("blk", "uly"), None),
        P(("blk", "uly"), None),
        P(("blk", "uly"), None),
        P("blk", None),
    )
    out_specs = (P(("blk", "uly"), None), P(("blk", "uly"), None), P(("blk", "uly"), None))
    return jax.shard_map(body, mesh=mesh, in_specs=in_specs, out_specs=out_specs, check_vma=False)
```

```python
import functools

import jax
import jax.numpy as jnp
from jax import lax
from jax.experimental import pallas as pl
from jax.experimental.pallas import tpu as pltpu
from jax.sharding import PartitionSpec as P

HD = 128
BLK = 128
CHB = 2
PIECES = 4
TEAM = 8
MESH = pl.DeviceIdType.MESH

loss_scale = 64.0
masked = -1e30
log2e = 1.4426950408889634


def dot(a, b, da, db):
    return lax.dot_general(a, b, (((da,), (db,)), ((), ())), preferred_element_type=jnp.float32)


def kernel(
    cfg,
    q_hbm, k_hbm, v_hbm, mask_ref,
    dq_hbm, dk_hbm, dv_hbm,
    qbuf, kbuf, vbuf, bbuf, bias_own, acc_k, acc_v,
    dq_st, dk_st, dv_st, gsend, grecv,
    f_send, f_recv, f_own, b_send, b_recv, m_sem,
    h_send, h_recv, r_send, r_recv, o_send, o_recv, o_own,
):
    span, ulys, teams, nh, halo, nb = cfg
    team = span * ulys
    rows = team * BLK
    hb = halo // BLK
    ch = CHB * BLK
    win = 2 * halo + ch
    wb = win // BLK
    nchunks = rows // ch
    scale = HD ** (-0.5)

    blk = lax.axis_index("blk")
    uly = lax.axis_index("uly")
    group = blk // span
    me = (blk % span) * ulys + uly
    has_lower = group > 0
    has_upper = group < teams - 1

    def device(index):
        return (group * span + index // ulys, index % ulys)

    lower = (blk - span, uly)
    upper = (blk + span, uly)

    barrier = pltpu.get_barrier_semaphore()

    def hello(d, _):
        pl.semaphore_signal(
            barrier, inc=1, device_id=device((me + d) % team), device_id_type=MESH
        )
        return 0

    lax.fori_loop(1, team, hello, 0)

    @pl.when(has_lower)
    def _():
        pl.semaphore_signal(barrier, inc=1, device_id=lower, device_id_type=MESH)

    @pl.when(has_upper)
    def _():
        pl.semaphore_signal(barrier, inc=1, device_id=upper, device_id_type=MESH)

    wpad = bias_own.shape[0]
    row_of = lax.broadcasted_iota(jnp.int32, mask_ref.shape, 0)
    own_row = jnp.sum(
        jnp.where(row_of == uly, mask_ref[...], 0).astype(jnp.float32), axis=0, keepdims=True
    )
    start = (group * team + (me // CHB) * CHB) - hb
    col = lax.broadcasted_iota(jnp.int32, (wpad, nb), 1)
    want = lax.broadcasted_iota(jnp.int32, (wpad, nb), 0) + start
    allowed = jnp.sum(
        jnp.where(col == want, jnp.broadcast_to(own_row, (wpad, nb)), 0.0), axis=1, keepdims=True
    )
    bias_own[...] = jnp.broadcast_to((1.0 - allowed) * masked, (wpad, BLK))

    beside = has_lower.astype(jnp.int32) + has_upper.astype(jnp.int32)
    pl.semaphore_wait(barrier, team - 1 + beside)

    my_rows = pl.multiple_of(me * BLK, BLK)

    def columns(owner, j):
        return pl.ds(pl.multiple_of((owner * nh + j) * HD, HD), HD)

    inputs = ((q_hbm, qbuf, 0), (k_hbm, kbuf, halo), (v_hbm, vbuf, halo))

    def push_mask(d, _):
        pltpu.make_async_remote_copy(
            src_ref=bias_own, dst_ref=bbuf.at[me], send_sem=b_send, recv_sem=b_recv,
            device_id=device((me + d) % team), device_id_type=MESH,
        ).start()
        return 0

    lax.fori_loop(1, team, push_mask, 0)

    def push_head(j, _):
        for a, (src, dst, offset) in enumerate(inputs):
            pltpu.make_async_copy(
                src.at[:, columns(me, j)],
                dst.at[j, pl.ds(my_rows + offset, BLK), :],
                f_own.at[a, j],
            ).start()

        def push_peer(d, _):
            peer = (me + d) % team
            for a, (src, dst, offset) in enumerate(inputs):
                pltpu.make_async_remote_copy(
                    src_ref=src.at[:, columns(peer, j)],
                    dst_ref=dst.at[j, pl.ds(my_rows + offset, BLK), :],
                    send_sem=f_send.at[a, j], recv_sem=f_recv.at[a, j],
                    device_id=device(peer), device_id_type=MESH,
                ).start()
            return 0

        lax.fori_loop(1, team, push_peer, 0)
        return 0

    lax.fori_loop(0, nh, push_head, 0)

    own_bias = pltpu.make_async_copy(bias_own, bbuf.at[me], m_sem)
    own_bias.start()
    own_bias.wait()

    acc_k[...] = jnp.zeros_like(acc_k)
    acc_v[...] = jnp.zeros_like(acc_v)
    edge = jnp.zeros((nh, halo, HD), jnp.bfloat16)

    @pl.when(jnp.logical_not(has_lower))
    def _():
        kbuf[:, 0:halo, :] = edge
        vbuf[:, 0:halo, :] = edge

    @pl.when(jnp.logical_not(has_upper))
    def _():
        kbuf[:, halo + rows :, :] = edge
        vbuf[:, halo + rows :, :] = edge

    def drain(ref, sem):
        pltpu.make_async_copy(ref, ref, sem).wait()

    peers_rows = (team - 1) * BLK
    drain(bbuf.at[pl.ds(0, team - 1)], b_recv)

    def halo_copies(j, side):
        place = halo if side == 0 else rows
        land = halo + rows if side == 0 else 0
        return [
            pltpu.make_async_remote_copy(
                src_ref=buf.at[j, pl.ds(place, halo), :],
                dst_ref=buf.at[j, pl.ds(land, halo), :],
                send_sem=h_send.at[a, j, side], recv_sem=h_recv.at[a, j, side],
                device_id=lower if side == 0 else upper, device_id_type=MESH,
            )
            for a, buf in enumerate((kbuf, vbuf))
        ]

    def grad_copies(j, side):
        return [
            pltpu.make_async_remote_copy(
                src_ref=gsend.at[a, j, side], dst_ref=grecv.at[a, j, side],
                send_sem=r_send.at[a, j, side], recv_sem=r_recv.at[a, j, side],
                device_id=lower if side == 0 else upper, device_id_type=MESH,
            )
            for a in range(2)
        ]

    there = (has_lower, has_upper)

    def send_block(a, j, block):
        st, out = ((dq_st, dq_hbm), (dk_st, dk_hbm), (dv_st, dv_hbm))[a]
        src = st.at[j, pl.ds(block * BLK, BLK), :]
        dst = out.at[:, columns(me, j)]

        @pl.when(me == block)
        def _():
            pltpu.make_async_copy(src, dst, o_own.at[a, j]).start()

        @pl.when(me != block)
        def _():
            pltpu.make_async_remote_copy(
                src_ref=src, dst_ref=dst, send_sem=o_send.at[a, j], recv_sem=o_recv.at[a, j],
                device_id=device(block), device_id_type=MESH,
            ).start()

    def chunk(j, c):
        base = c * ch
        k = kbuf[j, base : base + win, :]
        v = vbuf[j, base : base + win, :]
        q = qbuf[j, base : base + ch, :]
        bias = jnp.concatenate([bbuf[c * CHB + i] for i in range(CHB)], axis=1)[:wb]
        s = dot(k, q, 1, 1).reshape(wb, BLK, ch) * (scale * log2e) + bias[:, None, :]
        top = jnp.max(jnp.max(s, axis=0), axis=0, keepdims=True)
        p = jnp.exp2(s - top[None])
        total = jnp.sum(jnp.sum(p, axis=0), axis=0, keepdims=True)
        p = p.reshape(win, ch)
        pb = p.astype(jnp.bfloat16)
        inv = 1.0 / total
        o = dot(v, pb, 0, 0) * inv
        g = (loss_scale * o * inv).astype(jnp.bfloat16)
        delta = jnp.sum(g.astype(jnp.float32) * o, axis=0, keepdims=True)
        acc_v[j, base : base + win, :] += dot(pb, g, 1, 1)
        ds = (p * (dot(v, g, 1, 0) - delta)).astype(jnp.bfloat16)
        acc_k[j, base : base + win, :] += dot(ds, q, 1, 0)
        dq = dot(k, ds, 0, 0) * scale
        dq_st[j, base : base + ch, :] = dq.T.astype(jnp.bfloat16)
        for i in range(CHB):
            send_block(0, j, c * CHB + i)

    def finish_block(j, block):
        at = halo + block * BLK
        here = slice(block * BLK, (block + 1) * BLK)
        dk_st[j, here, :] = (acc_k[j, at : at + BLK, :] * scale).astype(jnp.bfloat16)
        dv_st[j, here, :] = acc_v[j, at : at + BLK, :].astype(jnp.bfloat16)
        send_block(1, j, block)
        send_block(2, j, block)

    inner_blocks = [b for b in range(team) if hb <= b < team - hb]
    outer_blocks = [b for b in range(team) if b not in inner_blocks]
    inner_chunks = [c for c in range(nchunks) if c * ch >= halo and c * ch + ch + halo <= rows]
    outer_chunks = [c for c in range(nchunks) if c not in inner_chunks]

    def finish_outer(j):
        for side in range(2):
            @pl.when(there[1 - side])
            def _():
                for copy in grad_copies(j, side):
                    copy.wait_recv()
                at = halo if side == 1 else rows
                acc_k[j, at : at + halo, :] += grecv[0, j, side].astype(jnp.float32)
                acc_v[j, at : at + halo, :] += grecv[1, j, side].astype(jnp.float32)

        for block in outer_blocks:
            finish_block(j, block)

    def head(j, _):
        for a, (src, dst, offset) in enumerate(inputs):
            drain(dst.at[j, pl.ds(offset, peers_rows), :], f_recv.at[a, j])
            drain(dst.at[j, pl.ds(offset, BLK), :], f_own.at[a, j])
        for side in range(2):
            @pl.when(there[side])
            def _():
                for copy in halo_copies(j, side):
                    copy.start()

        for c in inner_chunks:
            chunk(j, c)

        @pl.when(j > 0)
        def _():
            finish_outer(j - 1)

        for side in range(2):
            @pl.when(there[1 - side])
            def _():
                for copy in halo_copies(j, side):
                    copy.wait_recv()

        for c in outer_chunks:
            chunk(j, c)

        for side in range(2):
            @pl.when(there[side])
            def _():
                at = 0 if side == 0 else halo + rows
                gsend[0, j, side] = acc_k[j, at : at + halo, :].astype(jnp.bfloat16)
                gsend[1, j, side] = acc_v[j, at : at + halo, :].astype(jnp.bfloat16)
                for copy in grad_copies(j, side):
                    copy.start()

        for block in inner_blocks:
            finish_block(j, block)
        return 0

    lax.fori_loop(0, nh, head, 0)
    finish_outer(nh - 1)

    drain(bbuf.at[pl.ds(0, team - 1)], b_send)

    def settle(j, _):
        for a, (src, dst, offset) in enumerate(inputs):
            drain(dst.at[j, pl.ds(offset, peers_rows), :], f_send.at[a, j])
        for side in range(2):
            @pl.when(there[side])
            def _():
                for copy in halo_copies(j, side) + grad_copies(j, side):
                    copy.wait_send()

        for a, st in enumerate((dq_st, dk_st, dv_st)):
            drain(st.at[j, pl.ds(0, peers_rows), :], o_send.at[a, j])
            drain(st.at[j, pl.ds(0, BLK), :], o_own.at[a, j])
            drain(st.at[j, pl.ds(0, peers_rows), :], o_recv.at[a, j])
        return 0

    lax.fori_loop(0, nh, settle, 0)


def write_out(*refs):
    n = len(refs) // 2
    srcs, dsts, sem = refs[: n], refs[n : 2 * n], refs[2 * n]
    copies = []
    for a, (src, dst) in enumerate(zip(srcs, dsts)):
        step = src.shape[0] // PIECES
        for i in range(PIECES):
            here = pl.ds(i * step, step)
            copies.append(pltpu.make_async_copy(src.at[here], dst.at[here], sem.at[a, i]))
    for copy in copies:
        copy.start()
    for copy in copies:
        copy.wait()


def written(*arrays):
    anywhere = pl.BlockSpec(memory_space=pl.ANY)
    return pl.pallas_call(
        write_out,
        out_shape=[jax.ShapeDtypeStruct(a.shape, a.dtype) for a in arrays],
        in_specs=[anywhere] * len(arrays),
        out_specs=[pl.BlockSpec(memory_space=pltpu.HBM)] * len(arrays),
        scratch_shapes=[pltpu.SemaphoreType.DMA((len(arrays), PIECES))],
        compiler_params=pltpu.CompilerParams(vmem_limit_bytes=2 * 1024 * 1024),
    )(*arrays)


def body(query, keys, values, block_mask):
    blks = lax.axis_size("blk")
    ulys = lax.axis_size("uly")
    heads_all = query.shape[1] // HD
    span = max(1, TEAM // ulys)
    team = span * ulys
    nh = heads_all // team
    halo = query.shape[0] * ulys
    rows = team * BLK
    nb = block_mask.shape[1]
    cfg = (span, ulys, blks // span, nh, halo, nb)
    wpad = -(-(2 * halo // BLK + CHB) // 8) * 8
    grant = 51 if halo <= 2 * BLK else 56
    bf, f32 = jnp.bfloat16, jnp.float32
    dma = pltpu.SemaphoreType.DMA
    anywhere = pl.BlockSpec(memory_space=pl.ANY)
    grads = pl.pallas_call(
        functools.partial(kernel, cfg),
        out_shape=[jax.ShapeDtypeStruct(query.shape, bf)] * 3,
        in_specs=[pl.BlockSpec(memory_space=pltpu.HBM)] * 3 + [pl.BlockSpec(memory_space=pltpu.VMEM)],
        out_specs=[anywhere] * 3,
        scratch_shapes=[
            pltpu.VMEM((nh, rows, HD), bf),
            pltpu.VMEM((nh, rows + 2 * halo, HD), bf),
            pltpu.VMEM((nh, rows + 2 * halo, HD), bf),
            pltpu.VMEM((team, wpad, BLK), f32),
            pltpu.VMEM((wpad, BLK), f32),
            pltpu.VMEM((nh, rows + 2 * halo, HD), f32),
            pltpu.VMEM((nh, rows + 2 * halo, HD), f32),
            pltpu.VMEM((nh, rows, HD), bf),
            pltpu.VMEM((nh, rows, HD), bf),
            pltpu.VMEM((nh, rows, HD), bf),
            pltpu.VMEM((2, nh, 2, halo, HD), bf),
            pltpu.VMEM((2, nh, 2, halo, HD), bf),
            dma((3, nh)), dma((3, nh)), dma((3, nh)),
            dma, dma, dma,
            dma((2, nh, 2)), dma((2, nh, 2)), dma((2, nh, 2)), dma((2, nh, 2)),
            dma((3, nh)), dma((3, nh)), dma((3, nh)),
        ],
        compiler_params=pltpu.CompilerParams(
            collective_id=0, has_side_effects=True, vmem_limit_bytes=grant * 1024 * 1024
        ),
    )(query, keys, values, block_mask)
    return written(*grads)


def solution(mesh):
    in_specs = (
        P(("blk", "uly"), None),
        P(("blk", "uly"), None),
        P(("blk", "uly"), None),
        P("blk", None),
    )
    out_specs = (P(("blk", "uly"), None), P(("blk", "uly"), None), P(("blk", "uly"), None))
    return jax.shard_map(body, mesh=mesh, in_specs=in_specs, out_specs=out_specs, check_vma=False)
```
